32 devices in a mesh: pair: 8 (over z, x), cell: 4 (over y, core).
Axes of the slice: x: 2, y: 2, z: 4, core: 2. Of those that a mesh axis runs over, the one named last changes fastest.
Arguments:
- expression: bfloat16 [2048, 2048], P('cell', 'pair')
- plan: int32 [16], replicated, may hold values from 0 to 15, each once
- screen: int32 [4, 8], replicated, may hold values 0 or 1
Outputs:
- information: float32 [4, 1024, 128], P(None, ('pair', 'cell'))
The draws below stay inside these ranges and needn't reach their ends.
Inputs may be any that keep to these rules, and one draw needn't show every extreme that they name: `plan`: a permutation of the 16 block numbers.
All inputs are finite; a program needn't handle non-finite values.
Results may differ from the reference program's by a relative error of at most 0.0021.
Values may be sent and summed in bfloat16 or wider, within the bound.
A program may use at most 128 MiB of HBM per device.

```python
import jax
import jax.numpy as jnp
from jax import lax

BINS = 10
BLOCK = 128
ROUNDS = 4
CELLS = 2048
GENES = 2048
N_PAIR = 8
N_CELL = 4


def draw_expression(key, part):
    key = jax.random.fold_in(key, 11)
    keys = jax.random.split(key, 4)
    modules = jax.random.randint(keys[0], (GENES,), 0, 24)
    strength = jax.random.uniform(keys[1], (GENES,), jnp.float32, 0.35, 0.95)
    factors = jax.random.normal(keys[2], (CELLS, 24), jnp.float32)
    shared = jnp.take(factors, modules, axis=1)
    noise = jax.random.normal(keys[3], (CELLS, GENES), jnp.float32)
    values = strength * shared + jnp.sqrt(1.0 - strength * strength) * noise
    return jnp.clip(values, -8.0, 8.0).astype(jnp.bfloat16)


def touch_ends(array, stream_key, low, top_value):
    extent = array.shape
    spot = [jax.random.randint(jax.random.fold_in(stream_key, axis), (), 0, extent[axis]) for axis in range(len(extent))]
    array = array.at[tuple(spot)].set(low)
    longest = extent.index(max(extent))
    spot[longest] = (spot[longest] + 1) % extent[longest]
    return array.at[tuple(spot)].set(top_value)


def setup_inputs(seed: int = 0) -> dict:
    seeds = jax.random.split(jax.random.key(seed), 4)
    expression = draw_expression(jax.random.fold_in(seeds[3], 71), 0)
    plan = jax.random.permutation(seeds[1], 2 * N_PAIR).astype(jnp.int32)
    screen = touch_ends((jax.random.randint(seeds[2], (ROUNDS, N_PAIR), 0, 4) < 3).astype(jnp.int32), jax.random.fold_in(seeds[2], 1), 0, 1)
    return {"expression": expression, "plan": plan, "screen": screen}


def cubic_basis(scaled):
    top = float(BINS - 3)
    knot_list = [0.0, 0.0, 0.0] + [float(v) for v in range(BINS - 2)] + [top, top, top]
    level = [((scaled >= knot_list[i]) & (scaled < knot_list[i + 1])).astype(jnp.float32) for i in range(len(knot_list) - 1)]
    for k in range(2, 5):
        nextlevel = []
        for i in range(len(level) - 1):
            term = jnp.zeros_like(scaled)
            first_gap = knot_list[i + k - 1] - knot_list[i]
            if first_gap > 0:
                term = term + (scaled - knot_list[i]) / first_gap * level[i]
            second_gap = knot_list[i + k] - knot_list[i + 1]
            if second_gap > 0:
                term = term + (knot_list[i + k] - scaled) / second_gap * level[i + 1]
            nextlevel.append(term)
        level = nextlevel
    return level


def spline_weights(values):
    scaled = (BINS - 3) * jax.nn.sigmoid(values.astype(jnp.float32))
    basis = jnp.stack(cubic_basis(scaled), -1)
    return basis.reshape(values.shape[0], values.shape[1] * BINS).astype(jnp.bfloat16)


def entropy_terms(v):
    return v * jnp.log(jnp.maximum(v, 1e-30))


def mutual_information(histogram, cell_total):
    joint = histogram / cell_total
    genes_left = joint.shape[0] // BINS
    joint = joint.reshape(genes_left, BINS, BLOCK, BINS)
    whole = entropy_terms(joint).sum(axis=(1, 3))
    left = joint.sum(3)
    right = joint.sum(1)
    return whole - entropy_terms(left).sum(1) - entropy_terms(right).sum(2)


def reference(expression, plan, screen):
    cell_total = expression.shape[0]
    group_rows = cell_total // N_CELL
    seats = plan.reshape(N_PAIR, 2)
    firsts = seats[:, 0]
    seconds = seats[:, 1]

    def per_table(pair_blocks):
        first_block, second_block = pair_blocks
        first_values = lax.dynamic_slice_in_dim(expression, (first_block * BLOCK).astype(jnp.int32), BLOCK, 1)
        second_values = lax.dynamic_slice_in_dim(expression, (second_block * BLOCK).astype(jnp.int32), BLOCK, 1)
        first_weights = spline_weights(first_values).astype(jnp.float32).reshape(N_CELL, group_rows, BLOCK * BINS)
        second_weights = spline_weights(second_values).astype(jnp.float32).reshape(N_CELL, group_rows, BLOCK * BINS)
        partial_value = jnp.einsum("gca,gcb->gab", first_weights, second_weights)
        return mutual_information(partial_value.sum(0), cell_total)

    results = []
    for round_index in range(ROUNDS):
        if round_index > 0:
            new_firsts = jnp.concatenate([firsts[:1], seconds[:1], firsts[1:-1]])
            new_seconds = jnp.concatenate([seconds[1:], firsts[-1:]])
            firsts, seconds = new_firsts, new_seconds
        values = lax.map(per_table, (firsts, seconds))
        values = jnp.where(screen[round_index][:, None, None] == 1, values, jnp.float32(0.0))
        results.append(values.reshape(N_PAIR * BLOCK, BLOCK))
    return jnp.stack(results)
```

```python
import functools

import jax
import jax.numpy as jnp
import numpy as np
from jax import lax
from jax.experimental import pallas as pl
from jax.experimental.pallas import tpu as pltpu
from jax.sharding import PartitionSpec as P

BINS = 10
BLOCK = 128
ROUNDS = 4


def seat_table(tables):
    firsts = [2 * p for p in range(tables)]
    seconds = [2 * p + 1 for p in range(tables)]
    out = np.zeros((tables, ROUNDS, 2), np.int32)
    for r in range(ROUNDS):
        if r > 0:
            firsts, seconds = firsts[:1] + seconds[:1] + firsts[1:-1], seconds[1:] + firsts[-1:]
        out[:, r, 0] = firsts
        out[:, r, 1] = seconds
    return out


def basis(x, scale):
    s = 7.0 * jax.nn.sigmoid(x.astype(jnp.float32))
    k = jnp.floor(s)
    t = s - k
    n = 1.0 - t
    zero = jnp.zeros_like(s)
    m = [k == float(v) for v in range(7)]

    def side(t):
        t2 = t * t
        cube = t2 * t * scale
        edge1 = t * ((3.0 * scale) + t * ((-4.5 * scale) + (1.75 * scale) * t))
        edge2 = t2 * ((1.5 * scale) - (11.0 / 12.0 * scale) * t)
        return t2, cube, edge1, edge2

    t2, t3, e1, e2 = side(t)
    n2, n3, g1, g2 = side(n)
    t6 = t3 * (1.0 / 6.0)
    n6 = n3 * (1.0 / 6.0)
    fall = (2.0 / 3.0 * scale) - t2 * scale + 0.5 * t3
    rise = (2.0 / 3.0 * scale) - n2 * scale + 0.5 * n3
    h = 1.0 + n
    u = 1.0 + t
    e2b = h * h * h * (scale / 6.0) - 0.75 * n3
    g2b = u * u * u * (scale / 6.0) - 0.75 * t3
    t4 = 0.25 * t3
    n4 = 0.25 * n3

    def pick(*pairs):
        value = zero
        for mask, piece in pairs:
            value = jnp.where(mask, piece, value)
        return value

    return [
        pick((m[0], n3)),
        pick((m[0], e1), (m[1], n4)),
        pick((m[0], e2), (m[1], e2b), (m[2], n6)),
        pick((m[0], t6), (m[1], rise), (m[2], fall), (m[3], n6)),
        pick((m[1], t6), (m[2], rise), (m[3], fall), (m[4], n6)),
        pick((m[2], t6), (m[3], rise), (m[4], fall), (m[5], n6)),
        pick((m[3], t6), (m[4], rise), (m[5], fall), (m[6], n6)),
        pick((m[4], t6), (m[5], g2b), (m[6], g2)),
        pick((m[5], t4), (m[6], g1)),
        pick((m[6], t3)),
    ]


def entropy_terms(v):
    return v * jnp.log(jnp.maximum(v, 1e-30))


def kernel(first_ref, second_ref, out_ref, wf, ws, part, left):
    cells = second_ref.shape[0]

    @pl.loop(0, cells // 128)
    def _(c):
        at = pl.ds(pl.multiple_of(c * 128, 128), 128)
        for g in range(0, 128, 32):
            vals = basis(first_ref[g:g + 32, at], 1.0)
            for i in range(BINS):
                wf[i * BLOCK + g:i * BLOCK + g + 32, at] = vals[i].astype(jnp.bfloat16)

    @pl.loop(0, cells // 32)
    def _(c):
        at = pl.ds(pl.multiple_of(c * 32, 32), 32)
        vals = basis(second_ref[at, :], 1.0 / cells)
        for i in range(BINS):
            ws[at, i * BLOCK:(i + 1) * BLOCK] = vals[i].astype(jnp.bfloat16)

    out_ref[...] = jnp.zeros_like(out_ref)
    left[...] = jnp.zeros_like(left)
    for j in range(BINS // 2):
        part[...] = jnp.dot(
            wf[...], ws[:, j * 2 * BLOCK:(j + 1) * 2 * BLOCK], preferred_element_type=jnp.float32
        )

        @pl.loop(0, BLOCK // 16)
        def _(g):
            base = pl.multiple_of(g * 16, 16)
            total = out_ref[pl.ds(base, 16), :]
            right0 = jnp.zeros((16, BLOCK), jnp.float32)
            right1 = right0
            for i in range(BINS):
                rows = pl.ds(i * BLOCK + base, 16)
                v0 = part[rows, :BLOCK]
                v1 = part[rows, BLOCK:]
                total += entropy_terms(v0) + entropy_terms(v1)
                right0 += v0
                right1 += v1
                left[rows, :] += v0 + v1
            total -= entropy_terms(right0) + entropy_terms(right1)
            out_ref[pl.ds(base, 16), :] = total

    @pl.loop(0, BLOCK // 16)
    def _(g):
        base = pl.multiple_of(g * 16, 16)
        total = out_ref[pl.ds(base, 16), :]
        for i in range(BINS):
            total -= entropy_terms(left[pl.ds(i * BLOCK + base, 16), :])
        out_ref[pl.ds(base, 16), :] = total


def pair_information(first, second):
    cells = second.shape[0]
    return pl.pallas_call(
        kernel,
        out_shape=jax.ShapeDtypeStruct((BLOCK, BLOCK), jnp.float32),
        in_specs=[pl.BlockSpec(memory_space=pltpu.VMEM)] * 2,
        out_specs=pl.BlockSpec(memory_space=pltpu.VMEM),
        scratch_shapes=[
            pltpu.VMEM((BINS * BLOCK, cells), jnp.bfloat16),
            pltpu.VMEM((cells, BINS * BLOCK), jnp.bfloat16),
            pltpu.VMEM((BINS * BLOCK, 2 * BLOCK), jnp.float32),
            pltpu.VMEM((BINS * BLOCK, BLOCK), jnp.float32),
        ],
        compiler_params=pltpu.CompilerParams(vmem_limit_bytes=48 * 1024 * 1024),
    )(first, second)


def local(expression, plan, screen):
    tables = lax.axis_size("pair")
    groups = lax.axis_size("cell")
    split = groups // ROUNDS
    table = lax.axis_index("pair")
    group = lax.axis_index("cell")
    rows = expression.shape[0]
    cells = rows * groups
    seats = jnp.asarray(seat_table(tables))[table]
    wanted = plan[seats]
    blocks = expression.reshape(rows, 2, BLOCK).transpose(1, 0, 2)
    blocks = lax.all_gather(blocks, "pair", axis=0, tiled=True)
    order = [r // split for r in range(groups)]
    parts = []
    for c in range(groups):
        for s in range(2):
            parts.append(lax.dynamic_index_in_dim(blocks, wanted[order[c], s], 0, keepdims=False))
    send = jnp.stack(parts).reshape(groups, 2, rows, BLOCK)
    got = lax.all_to_all(send, "cell", 0, 0, tiled=True)
    first = got[:, 0].reshape(cells, BLOCK).T
    second = got[:, 1].reshape(cells, BLOCK)
    mine = pair_information(first, second)
    mine = jnp.where(screen[group // split, table] == 1, mine, jnp.float32(0.0))
    share = BLOCK // groups
    if split == 1:
        return lax.all_to_all(mine.reshape(groups, share, BLOCK), "cell", 0, 0, tiled=True)
    every = lax.all_gather(mine, "cell", axis=0)[::split]
    return lax.dynamic_slice_in_dim(every, group * share, share, 1)


def solution(mesh):
    return jax.shard_map(
        local,
        mesh=mesh,
        in_specs=(P("cell", "pair"), P(), P()),
        out_specs=P(None, ("pair", "cell"), None),
        check_vma=False,
    )
```

```python
import functools

import jax
import jax.numpy as jnp
import numpy as np
from jax import lax
from jax.experimental import pallas as pl
from jax.experimental.pallas import tpu as pltpu
from jax.sharding import PartitionSpec as P

BINS = 10
BLOCK = 128
ROUNDS = 4


def seat_table(tables):
    firsts = [2 * p for p in range(tables)]
    seconds = [2 * p + 1 for p in range(tables)]
    out = np.zeros((tables, ROUNDS, 2), np.int32)
    for r in range(ROUNDS):
        if r > 0:
            firsts, seconds = firsts[:1] + seconds[:1] + firsts[1:-1], seconds[1:] + firsts[-1:]
        out[:, r, 0] = firsts
        out[:, r, 1] = seconds
    return out


def basis(x, scale):
    s = 7.0 * jax.nn.sigmoid(x.astype(jnp.float32))
    k = jnp.floor(s)
    t = s - k
    n = 1.0 - t
    zero = jnp.zeros_like(s)
    m = [k == float(v) for v in range(7)]

    def side(t):
        t2 = t * t
        cube = t2 * t * scale
        edge1 = t * ((3.0 * scale) + t * ((-4.5 * scale) + (1.75 * scale) * t))
        edge2 = t2 * ((1.5 * scale) - (11.0 / 12.0 * scale) * t)
        return t2, cube, edge1, edge2

    t2, t3, e1, e2 = side(t)
    n2, n3, g1, g2 = side(n)
    t6 = t3 * (1.0 / 6.0)
    n6 = n3 * (1.0 / 6.0)
    fall = (2.0 / 3.0 * scale) - t2 * scale + 0.5 * t3
    rise = (2.0 / 3.0 * scale) - n2 * scale + 0.5 * n3
    h = 1.0 + n
    u = 1.0 + t
    e2b = h * h * h * (scale / 6.0) - 0.75 * n3
    g2b = u * u * u * (scale / 6.0) - 0.75 * t3
    t4 = 0.25 * t3
    n4 = 0.25 * n3

    def pick(*pairs):
        value = zero
        for mask, piece in pairs:
            value = jnp.where(mask, piece, value)
        return value

    return [
        pick((m[0], n3)),
        pick((m[0], e1), (m[1], n4)),
        pick((m[0], e2), (m[1], e2b), (m[2], n6)),
        pick((m[0], t6), (m[1], rise), (m[2], fall), (m[3], n6)),
        pick((m[1], t6), (m[2], rise), (m[3], fall), (m[4], n6)),
        pick((m[2], t6), (m[3], rise), (m[4], fall), (m[5], n6)),
        pick((m[3], t6), (m[4], rise), (m[5], fall), (m[6], n6)),
        pick((m[4], t6), (m[5], g2b), (m[6], g2)),
        pick((m[5], t4), (m[6], g1)),
        pick((m[6], t3)),
    ]


def entropy_terms(v):
    return v * jnp.log(jnp.maximum(v, 1e-30))


def grid_of(tables):
    columns = 1
    while 2 * (2 * columns) * (2 * columns) <= tables and tables % (2 * columns) == 0:
        columns *= 2
    return tables // columns, columns


def route(tables, groups, pieces, wanted_ref, expr_ref, out_ref, *scratch):
    gath = scratch[:pieces]
    chosen, z_send, z_recv, x_send, x_recv, c_send, c_recv = scratch[pieces:]
    zs, xs = grid_of(tables)
    split = groups // ROUNDS
    me = lax.axis_index("pair")
    group = lax.axis_index("cell")
    z = lax.div(me, xs)
    x = lax.rem(me, xs)
    rows = expr_ref.shape[0]
    part = rows // pieces
    mesh_id = pl.DeviceIdType.MESH

    def own_pair(ch):
        return gath[ch].at[pl.ds(2 * me, 2)]

    def z_copy(ch, step, up, owner_z, to_z):
        ref = gath[ch].at[pl.ds(2 * (owner_z * xs + x), 2)]
        return pltpu.make_async_remote_copy(
            src_ref=ref, dst_ref=ref,
            send_sem=z_send.at[up, ch, step], recv_sem=z_recv.at[up, ch, step],
            device_id=(to_z * xs + x, group), device_id_type=mesh_id,
        )

    def up_out(ch, step):
        return (z + 1 < zs) & (z - step + 1 >= 0), z_copy(ch, step, 1, z - step + 1, z + 1)

    def down_out(ch, step):
        return (z >= 1) & (z + step - 1 < zs), z_copy(ch, step, 0, z + step - 1, z - 1)

    def up_in(ch, step):
        return z - step >= 0, z_copy(ch, step, 1, z - step, z - 1)

    def down_in(ch, step):
        return z + step < zs, z_copy(ch, step, 0, z + step, z + 1)

    def x_copy(ch, owner_z, owner_x, d):
        ref = gath[ch].at[pl.ds(2 * (owner_z * xs + owner_x), 2)]
        return pltpu.make_async_remote_copy(
            src_ref=ref, dst_ref=ref,
            send_sem=x_send.at[ch, owner_z, d], recv_sem=x_recv.at[ch, owner_z, d],
            device_id=(z * xs + lax.rem(x + d, xs), group), device_id_type=mesh_id,
        )

    def c_copy(ch, d):
        to = lax.rem(group + d, groups)
        return pltpu.make_async_remote_copy(
            src_ref=chosen.at[ch, to],
            dst_ref=out_ref.at[:, pl.ds(pl.multiple_of(group * rows + ch * part, part), part)],
            send_sem=c_send.at[ch, d], recv_sem=c_recv.at[ch, d],
            device_id=(me, to), device_id_type=mesh_id,
        )

    def share_row(ch, owner_z):
        for d in range(1, xs):
            x_copy(ch, owner_z, x, d).start()

    barrier = pltpu.get_barrier_semaphore()

    @pl.when(z >= 1)
    def _():
        pl.semaphore_signal(barrier, inc=1, device_id=(me - xs, group), device_id_type=mesh_id)

    @pl.when(z + 1 < zs)
    def _():
        pl.semaphore_signal(barrier, inc=1, device_id=(me + xs, group), device_id_type=mesh_id)

    for d in range(1, xs):
        pl.semaphore_signal(
            barrier, inc=1, device_id=(z * xs + lax.rem(x + d, xs), group), device_id_type=mesh_id
        )
    for d in range(1, groups):
        pl.semaphore_signal(
            barrier, inc=1, device_id=(me, lax.rem(group + d, groups)), device_id_type=mesh_id
        )
    for ch in range(pieces):
        for h in range(2):
            gath[ch][2 * me + h] = expr_ref[ch * part:(ch + 1) * part, h * BLOCK:(h + 1) * BLOCK]
    z_peers = lax.div(z + zs - 1, zs) + lax.div(2 * zs - 2 - z, zs)
    pl.semaphore_wait(barrier, xs + groups - 2 + z_peers)

    def begin(copy_if):
        cond, copy = copy_if

        @pl.when(cond)
        def _():
            copy.start()

    def advance(ch, step):
        if step == 0:
            begin(up_out(ch, 1))
            begin(down_out(ch, 1))
            share_row(ch, z)
            return
        for arrive, leave, owner in ((up_in, up_out, z - step), (down_in, down_out, z + step)):
            cond, copy = arrive(ch, step)

            @pl.when(cond)
            def _():
                copy.wait_recv()
                if step + 1 < zs:
                    begin(leave(ch, step + 1))
                share_row(ch, owner)

    def choose(ch):
        for owner_z in range(zs):
            for d in range(1, xs):
                x_copy(ch, owner_z, lax.rem(x + xs - d, xs), d).wait_recv()
        for c in range(groups):
            for s in range(2):
                chosen[ch, c, s] = gath[ch][wanted_ref[2 * (c // split) + s]]
        for d in range(1, groups):
            c_copy(ch, d).start()
        out_ref[:, pl.ds(pl.multiple_of(group * rows + ch * part, part), part)] = chosen[ch, group]

    for tick in range(pieces + zs - 1):
        for ch in range(pieces):
            if 0 <= tick - ch < zs:
                advance(ch, tick - ch)
        if tick >= zs - 1:
            choose(tick - zs + 1)

    for ch in range(pieces):
        for d in range(1, groups):
            c_copy(ch, d).wait_send()
            c_copy(ch, d).wait_recv()
        for step in range(1, zs):
            for cond, copy in (up_out(ch, step), down_out(ch, step)):

                @pl.when(cond)
                def _():
                    copy.wait_send()
        for owner_z in range(zs):
            for d in range(1, xs):
                x_copy(ch, owner_z, x, d).wait_send()


def seat_blocks(expression, wanted, tables, groups):
    rows = expression.shape[0]
    zs, xs = grid_of(tables)
    pieces = 4
    part = rows // pieces
    dma = pltpu.SemaphoreType.DMA
    return pl.pallas_call(
        functools.partial(route, tables, groups, pieces),
        out_shape=jax.ShapeDtypeStruct((2, rows * groups, BLOCK), jnp.bfloat16),
        in_specs=[
            pl.BlockSpec(memory_space=pltpu.SMEM),
            pl.BlockSpec(memory_space=pltpu.VMEM),
        ],
        out_specs=pl.BlockSpec(memory_space=pltpu.VMEM),
        scratch_shapes=[pltpu.VMEM((2 * tables, part, BLOCK), jnp.bfloat16)] * pieces
        + [
            pltpu.VMEM((pieces, groups, 2, part, BLOCK), jnp.bfloat16),
            dma((2, pieces, zs)),
            dma((2, pieces, zs)),
            dma((pieces, zs, xs)),
            dma((pieces, zs, xs)),
            dma((pieces, groups)),
            dma((pieces, groups)),
        ],
        compiler_params=pltpu.CompilerParams(
            collective_id=0, has_side_effects=True, vmem_limit_bytes=40 * 1024 * 1024
        ),
    )(wanted, expression)


def kernel(x_ref, out_ref, wf, ws, part, left):
    cells = x_ref.shape[1]

    @pl.loop(0, cells // 128)
    def _(c):
        at = pl.ds(pl.multiple_of(c * 128, 128), 128)
        turned = x_ref[0, at, :].astype(jnp.float32).T
        for g in range(0, 128, 32):
            vals = basis(turned[g:g + 32], 1.0)
            for i in range(BINS):
                wf[i * BLOCK + g:i * BLOCK + g + 32, at] = vals[i].astype(jnp.bfloat16)

    @pl.loop(0, cells // 32)
    def _(c):
        at = pl.ds(pl.multiple_of(c * 32, 32), 32)
        vals = basis(x_ref[1, at, :], 1.0 / cells)
        for i in range(BINS):
            ws[at, i * BLOCK:(i + 1) * BLOCK] = vals[i].astype(jnp.bfloat16)

    out_ref[...] = jnp.zeros_like(out_ref)
    left[...] = jnp.zeros_like(left)
    for j in range(BINS // 2):
        part[...] = jnp.dot(
            wf[...], ws[:, j * 2 * BLOCK:(j + 1) * 2 * BLOCK], preferred_element_type=jnp.float32
        )

        @pl.loop(0, BLOCK // 16)
        def _(g):
            base = pl.multiple_of(g * 16, 16)
            total = out_ref[pl.ds(base, 16), :]
            right0 = jnp.zeros((16, BLOCK), jnp.float32)
            right1 = right0
            for i in range(BINS):
                rows = pl.ds(i * BLOCK + base, 16)
                v0 = part[rows, :BLOCK]
                v1 = part[rows, BLOCK:]
                total += entropy_terms(v0) + entropy_terms(v1)
                right0 += v0
                right1 += v1
                left[rows, :] += v0 + v1
            total -= entropy_terms(right0) + entropy_terms(right1)
            out_ref[pl.ds(base, 16), :] = total

    @pl.loop(0, BLOCK // 16)
    def _(g):
        base = pl.multiple_of(g * 16, 16)
        total = out_ref[pl.ds(base, 16), :]
        for i in range(BINS):
            total -= entropy_terms(left[pl.ds(i * BLOCK + base, 16), :])
        out_ref[pl.ds(base, 16), :] = total


def pair_information(blocks):
    cells = blocks.shape[1]
    return pl.pallas_call(
        kernel,
        out_shape=jax.ShapeDtypeStruct((BLOCK, BLOCK), jnp.float32),
        in_specs=[pl.BlockSpec(memory_space=pltpu.VMEM)],
        out_specs=pl.BlockSpec(memory_space=pltpu.VMEM),
        scratch_shapes=[
            pltpu.VMEM((BINS * BLOCK, cells), jnp.bfloat16),
            pltpu.VMEM((cells, BINS * BLOCK), jnp.bfloat16),
            pltpu.VMEM((BINS * BLOCK, 2 * BLOCK), jnp.float32),
            pltpu.VMEM((BINS * BLOCK, BLOCK), jnp.float32),
        ],
        compiler_params=pltpu.CompilerParams(vmem_limit_bytes=48 * 1024 * 1024),
    )(blocks)


def local(expression, plan, screen):
    tables = lax.axis_size("pair")
    groups = lax.axis_size("cell")
    split = groups // ROUNDS
    table = lax.axis_index("pair")
    group = lax.axis_index("cell")
    seats = jnp.asarray(seat_table(tables))[table]
    wanted = plan[seats].reshape(2 * ROUNDS)
    mine = pair_information(seat_blocks(expression, wanted, tables, groups))
    mine = jnp.where(screen[group // split, table] == 1, mine, jnp.float32(0.0))
    share = BLOCK // groups
    if split == 1:
        return lax.all_to_all(mine.reshape(groups, share, BLOCK), "cell", 0, 0, tiled=True)
    every = lax.all_gather(mine, "cell", axis=0)[::split]
    return lax.dynamic_slice_in_dim(every, group * share, share, 1)


def solution(mesh):
    return jax.shard_map(
        local,
        mesh=mesh,
        in_specs=(P("cell", "pair"), P(), P()),
        out_specs=P(None, ("pair", "cell"), None),
        check_vma=False,
    )
```

```python
import functools

import jax
import jax.numpy as jnp
from jax import lax
from jax.experimental import pallas as pl
from jax.experimental.pallas import tpu as pltpu
from jax.sharding import PartitionSpec as P

BINS = 10
BLOCK = 128
ROUNDS = 4


def seat_of(tables, table, turn):
    ring = 2 * tables - 1

    def start(place):
        was = lax.rem(place + ring - turn, ring)
        other = 2 * lax.rem(ring - was, ring) + 1
        return jnp.where((was >= 1) & (was < tables), 2 * was, other)

    first = jnp.where(table == 0, 0, start(table))
    return first, start(lax.rem(ring - table, ring))


def basis(x, scale):
    s = 7.0 * jax.nn.sigmoid(x.astype(jnp.float32))
    k = jnp.floor(s)
    t = s - k
    n = 1.0 - t
    zero = jnp.zeros_like(s)
    m = [k == float(v) for v in range(7)]

    def side(t):
        t2 = t * t
        cube = t2 * t * scale
        edge1 = t * ((3.0 * scale) + t * ((-4.5 * scale) + (1.75 * scale) * t))
        edge2 = t2 * ((1.5 * scale) - (11.0 / 12.0 * scale) * t)
        return t2, cube, edge1, edge2

    t2, t3, e1, e2 = side(t)
    n2, n3, g1, g2 = side(n)
    t6 = t3 * (1.0 / 6.0)
    n6 = n3 * (1.0 / 6.0)
    fall = (2.0 / 3.0 * scale) - t2 * scale + 0.5 * t3
    rise = (2.0 / 3.0 * scale) - n2 * scale + 0.5 * n3
    h = 1.0 + n
    u = 1.0 + t
    e2b = h * h * h * (scale / 6.0) - 0.75 * n3
    g2b = u * u * u * (scale / 6.0) - 0.75 * t3
    t4 = 0.25 * t3
    n4 = 0.25 * n3

    def pick(*pairs):
        value = zero
        for mask, piece in pairs:
            value = jnp.where(mask, piece, value)
        return value

    return [
        pick((m[0], n3)),
        pick((m[0], e1), (m[1], n4)),
        pick((m[0], e2), (m[1], e2b), (m[2], n6)),
        pick((m[0], t6), (m[1], rise), (m[2], fall), (m[3], n6)),
        pick((m[1], t6), (m[2], rise), (m[3], fall), (m[4], n6)),
        pick((m[2], t6), (m[3], rise), (m[4], fall), (m[5], n6)),
        pick((m[3], t6), (m[4], rise), (m[5], fall), (m[6], n6)),
        pick((m[4], t6), (m[5], g2b), (m[6], g2)),
        pick((m[5], t4), (m[6], g1)),
        pick((m[6], t3)),
    ]


def entropy_terms(v):
    return v * jnp.log(jnp.maximum(v, 1e-30))


def grid_of(tables):
    columns = 1
    while 2 * (2 * columns) * (2 * columns) <= tables and tables % (2 * columns) == 0:
        columns *= 2
    return tables // columns, columns


def kernel(tables, groups, pieces, plan_ref, expr_ref, out_ref, *scratch):
    gath = scratch[:pieces]
    chosen, seated, wf, ws, part_sums, left, mine = scratch[pieces:pieces + 7]
    z_send, z_recv, x_send, x_recv, c_send, c_recv, o_send, o_recv = scratch[pieces + 7:]
    zs, xs = grid_of(tables)
    split = groups // ROUNDS
    me = lax.axis_index("pair")
    group = lax.axis_index("cell")
    z = lax.div(me, xs)
    x = lax.rem(me, xs)
    rows = expr_ref.shape[0]
    part = rows // pieces
    mesh_id = pl.DeviceIdType.MESH

    def own_pair(ch):
        return gath[ch].at[pl.ds(2 * me, 2)]

    def z_copy(ch, step, up, owner_z, to_z):
        ref = gath[ch].at[pl.ds(2 * (owner_z * xs + x), 2)]
        return pltpu.make_async_remote_copy(
            src_ref=ref, dst_ref=ref,
            send_sem=z_send.at[up, ch, step], recv_sem=z_recv.at[up, ch, step],
            device_id=(to_z * xs + x, group), device_id_type=mesh_id,
        )

    def up_out(ch, step):
        return (z + 1 < zs) & (z - step + 1 >= 0), z_copy(ch, step, 1, z - step + 1, z + 1)

    def down_out(ch, step):
        return (z >= 1) & (z + step - 1 < zs), z_copy(ch, step, 0, z + step - 1, z - 1)

    def up_in(ch, step):
        return z - step >= 0, z_copy(ch, step, 1, z - step, z - 1)

    def down_in(ch, step):
        return z + step < zs, z_copy(ch, step, 0, z + step, z + 1)

    def x_copy(ch, owner_z, owner_x, d):
        ref = gath[ch].at[pl.ds(2 * (owner_z * xs + owner_x), 2)]
        return pltpu.make_async_remote_copy(
            src_ref=ref, dst_ref=ref,
            send_sem=x_send.at[ch, owner_z, d], recv_sem=x_recv.at[ch, owner_z, d],
            device_id=(z * xs + lax.rem(x + d, xs), group), device_id_type=mesh_id,
        )

    def c_copy(ch, d):
        to = lax.rem(group + d, groups)
        return pltpu.make_async_remote_copy(
            src_ref=chosen.at[ch, to],
            dst_ref=seated.at[:, pl.ds(pl.multiple_of(group * rows + ch * part, part), part)],
            send_sem=c_send.at[ch, d], recv_sem=c_recv.at[ch, d],
            device_id=(me, to), device_id_type=mesh_id,
        )

    def share_row(ch, owner_z):
        for d in range(1, xs):
            x_copy(ch, owner_z, x, d).start()

    barrier = pltpu.get_barrier_semaphore()

    @pl.when(z >= 1)
    def _():
        pl.semaphore_signal(barrier, inc=1, device_id=(me - xs, group), device_id_type=mesh_id)

    @pl.when(z + 1 < zs)
    def _():
        pl.semaphore_signal(barrier, inc=1, device_id=(me + xs, group), device_id_type=mesh_id)

    for d in range(1, xs):
        pl.semaphore_signal(
            barrier, inc=1, device_id=(z * xs + lax.rem(x + d, xs), group), device_id_type=mesh_id
        )
    for d in range(1, groups):
        pl.semaphore_signal(
            barrier, inc=1, device_id=(me, lax.rem(group + d, groups)), device_id_type=mesh_id
        )
    for ch in range(pieces):
        for h in range(2):
            gath[ch][2 * me + h] = expr_ref[ch * part:(ch + 1) * part, h * BLOCK:(h + 1) * BLOCK]
    z_peers = lax.div(z + zs - 1, zs) + lax.div(2 * zs - 2 - z, zs)
    pl.semaphore_wait(barrier, xs + groups - 2 + z_peers)

    def begin(copy_if):
        cond, copy = copy_if

        @pl.when(cond)
        def _():
            copy.start()

    def advance(ch, step):
        if step == 0:
            begin(up_out(ch, 1))
            begin(down_out(ch, 1))
            share_row(ch, z)
            return
        for arrive, leave, owner in ((up_in, up_out, z - step), (down_in, down_out, z + step)):
            cond, copy = arrive(ch, step)

            @pl.when(cond)
            def _():
                copy.wait_recv()
                if step + 1 < zs:
                    begin(leave(ch, step + 1))
                share_row(ch, owner)

    def choose(ch):
        for owner_z in range(zs):
            for d in range(1, xs):
                x_copy(ch, owner_z, lax.rem(x + xs - d, xs), d).wait_recv()
        for c in range(groups):
            for s, seat in enumerate(seat_of(tables, me, c // split)):
                chosen[ch, c, s] = gath[ch][plan_ref[seat]]
        for d in range(1, groups):
            c_copy(ch, d).start()
        seated[:, pl.ds(pl.multiple_of(group * rows + ch * part, part), part)] = chosen[ch, group]

    def weigh(ch):
        for d in range(1, groups):
            c_copy(ch, d).wait_recv()

        @pl.loop(0, groups)
        def _(g):
            base = pl.multiple_of(g * rows + ch * part, part)
            at = pl.ds(base, part)
            turned = seated[0, at, :].astype(jnp.float32).T
            for k in range(0, BLOCK, 32):
                vals = basis(turned[k:k + 32], 1.0)
                for i in range(BINS):
                    wf[i * BLOCK + k:i * BLOCK + k + 32, at] = vals[i].astype(jnp.bfloat16)
            for k in range(0, part, 32):
                rows_at = pl.ds(base + k, 32)
                vals = basis(seated[1, rows_at, :], 1.0 / (rows * groups))
                for i in range(BINS):
                    ws[rows_at, i * BLOCK:(i + 1) * BLOCK] = vals[i].astype(jnp.bfloat16)

    for tick in range(pieces + zs + 1):
        for ch in range(pieces):
            if 0 <= tick - ch < zs:
                advance(ch, tick - ch)
        if 0 <= tick - zs < pieces:
            choose(tick - zs)
        if 0 <= tick - zs - 1 < pieces:
            weigh(tick - zs - 1)

    mine[...] = jnp.zeros_like(mine)
    left[...] = jnp.zeros_like(left)
    for j in range(BINS // 2):
        part_sums[...] = jnp.dot(
            wf[...], ws[:, j * 2 * BLOCK:(j + 1) * 2 * BLOCK], preferred_element_type=jnp.float32
        )

        @pl.loop(0, BLOCK // 16)
        def _(g):
            base = pl.multiple_of(g * 16, 16)
            total = mine[pl.ds(base, 16), :]
            right0 = jnp.zeros((16, BLOCK), jnp.float32)
            right1 = right0
            for i in range(BINS):
                rows = pl.ds(i * BLOCK + base, 16)
                v0 = part_sums[rows, :BLOCK]
                v1 = part_sums[rows, BLOCK:]
                total += entropy_terms(v0) + entropy_terms(v1)
                right0 += v0
                right1 += v1
                left[rows, :] += v0 + v1
            total -= entropy_terms(right0) + entropy_terms(right1)
            mine[pl.ds(base, 16), :] = total

    @pl.loop(0, BLOCK // 16)
    def _(g):
        base = pl.multiple_of(g * 16, 16)
        total = mine[pl.ds(base, 16), :]
        for i in range(BINS):
            total -= entropy_terms(left[pl.ds(i * BLOCK + base, 16), :])
        mine[pl.ds(base, 16), :] = total

    share = out_ref.shape[1]
    turn = lax.div(group, split)

    def o_copy(k):
        to = lax.rem(group + k * split, groups)
        return pltpu.make_async_remote_copy(
            src_ref=mine.at[pl.ds(pl.multiple_of(to * share, share), share)],
            dst_ref=out_ref.at[turn],
            send_sem=o_send.at[k], recv_sem=o_recv.at[k],
            device_id=(me, to), device_id_type=mesh_id,
        )

    for k in range(1, ROUNDS):
        o_copy(k).start()
    out_ref[turn] = mine[pl.ds(pl.multiple_of(group * share, share), share), :]
    for ch in range(pieces):
        for d in range(1, groups):
            c_copy(ch, d).wait_send()
        for step in range(1, zs):
            for cond, copy in (up_out(ch, step), down_out(ch, step)):

                @pl.when(cond)
                def _():
                    copy.wait_send()
        for owner_z in range(zs):
            for d in range(1, xs):
                x_copy(ch, owner_z, x, d).wait_send()
    for k in range(1, ROUNDS):
        o_copy(k).wait()


def local(expression, plan, screen):
    tables = lax.axis_size("pair")
    groups = lax.axis_size("cell")
    rows = expression.shape[0]
    cells = rows * groups
    zs, xs = grid_of(tables)
    pieces = rows // BLOCK
    part = rows // pieces
    dma = pltpu.SemaphoreType.DMA
    values = pl.pallas_call(
        functools.partial(kernel, tables, groups, pieces),
        out_shape=jax.ShapeDtypeStruct((ROUNDS, BLOCK // groups, BLOCK), jnp.float32),
        in_specs=[
            pl.BlockSpec(memory_space=pltpu.SMEM),
            pl.BlockSpec(memory_space=pltpu.VMEM),
        ],
        out_specs=pl.BlockSpec(memory_space=pltpu.VMEM),
        scratch_shapes=[pltpu.VMEM((2 * tables, part, BLOCK), jnp.bfloat16)] * pieces
        + [
            pltpu.VMEM((pieces, groups, 2, part, BLOCK), jnp.bfloat16),
            pltpu.VMEM((2, cells, BLOCK), jnp.bfloat16),
            pltpu.VMEM((BINS * BLOCK, cells), jnp.bfloat16),
            pltpu.VMEM((cells, BINS * BLOCK), jnp.bfloat16),
            pltpu.VMEM((BINS * BLOCK, 2 * BLOCK), jnp.float32),
            pltpu.VMEM((BINS * BLOCK, BLOCK), jnp.float32),
            pltpu.VMEM((BLOCK, BLOCK), jnp.float32),
            dma((2, pieces, zs)),
            dma((2, pieces, zs)),
            dma((pieces, zs, xs)),
            dma((pieces, zs, xs)),
            dma((pieces, groups)),
            dma((pieces, groups)),
            dma((ROUNDS,)),
            dma((ROUNDS,)),
        ],
        compiler_params=pltpu.CompilerParams(
            collective_id=0, has_side_effects=True, vmem_limit_bytes=52 * 1024 * 1024
        ),
    )(plan, expression)
    passed = lax.dynamic_slice_in_dim(screen, lax.axis_index("pair"), 1, 1)
    return jnp.where(passed[:, :, None] == 1, values, jnp.float32(0.0))


def solution(mesh):
    return jax.shard_map(
        local,
        mesh=mesh,
        in_specs=(P("cell", "pair"), P(), P()),
        out_specs=P(None, ("pair", "cell"), None),
        check_vma=False,
    )
```

```python
import functools

import jax
import jax.numpy as jnp
from jax import lax
from jax.experimental import pallas as pl
from jax.experimental.pallas import tpu as pltpu
from jax.sharding import PartitionSpec as P

BINS = 10
BLOCK = 128
ROUNDS = 4


def seat_of(tables, table, turn):
    ring = 2 * tables - 1

    def start(place):
        was = lax.rem(place + ring - turn, ring)
        other = 2 * lax.rem(ring - was, ring) + 1
        return jnp.where((was >= 1) & (was < tables), 2 * was, other)

    first = jnp.where(table == 0, 0, start(table))
    return first, start(lax.rem(ring - table, ring))


def basis(x, scale):
    s = 7.0 * jax.nn.sigmoid(x.astype(jnp.float32))
    k = jnp.floor(s)
    t = s - k
    n = 1.0 - t
    zero = jnp.zeros_like(s)
    m = [k == float(v) for v in range(7)]

    def side(t):
        t2 = t * t
        cube = t2 * t * scale
        edge1 = t * ((3.0 * scale) + t * ((-4.5 * scale) + (1.75 * scale) * t))
        edge2 = t2 * ((1.5 * scale) - (11.0 / 12.0 * scale) * t)
        return t2, cube, edge1, edge2

    t2, t3, e1, e2 = side(t)
    n2, n3, g1, g2 = side(n)
    t6 = t3 * (1.0 / 6.0)
    n6 = n3 * (1.0 / 6.0)
    fall = (2.0 / 3.0 * scale) - t2 * scale + 0.5 * t3
    rise = (2.0 / 3.0 * scale) - n2 * scale + 0.5 * n3
    h = 1.0 + n
    u = 1.0 + t
    e2b = h * h * h * (scale / 6.0) - 0.75 * n3
    g2b = u * u * u * (scale / 6.0) - 0.75 * t3
    t4 = 0.25 * t3
    n4 = 0.25 * n3

    def pick(*pairs):
        value = zero
        for mask, piece in pairs:
            value = jnp.where(mask, piece, value)
        return value

    return [
        pick((m[0], n3)),
        pick((m[0], e1), (m[1], n4)),
        pick((m[0], e2), (m[1], e2b), (m[2], n6)),
        pick((m[0], t6), (m[1], rise), (m[2], fall), (m[3], n6)),
        pick((m[1], t6), (m[2], rise), (m[3], fall), (m[4], n6)),
        pick((m[2], t6), (m[3], rise), (m[4], fall), (m[5], n6)),
        pick((m[3], t6), (m[4], rise), (m[5], fall), (m[6], n6)),
        pick((m[4], t6), (m[5], g2b), (m[6], g2)),
        pick((m[5], t4), (m[6], g1)),
        pick((m[6], t3)),
    ]


def entropy_terms(v):
    return v * jnp.log(jnp.maximum(v, 1e-30))


def grid_of(tables):
    columns = 1
    while 2 * (2 * columns) * (2 * columns) <= tables and tables % (2 * columns) == 0:
        columns *= 2
    return tables // columns, columns


def kernel(tables, groups, pieces, plan_ref, expr_ref, out_ref, *scratch):
    gath = scratch[:pieces]
    chosen, seated, wf, ws, part_sums, left, mine = scratch[pieces:pieces + 7]
    z_send, z_recv, x_send, x_recv, c_send, c_recv, o_send, o_recv = scratch[pieces + 7:]
    zs, xs = grid_of(tables)
    split = groups // ROUNDS
    me = lax.axis_index("pair")
    group = lax.axis_index("cell")
    z = lax.div(me, xs)
    x = lax.rem(me, xs)
    rows = expr_ref.shape[0]
    part = rows // pieces
    mesh_id = pl.DeviceIdType.MESH

    def own_pair(ch):
        return gath[ch].at[pl.ds(2 * me, 2)]

    def z_copy(ch, step, up, owner_z, to_z):
        ref = gath[ch].at[pl.ds(2 * (owner_z * xs + x), 2)]
        return pltpu.make_async_remote_copy(
            src_ref=ref, dst_ref=ref,
            send_sem=z_send.at[up, ch, step], recv_sem=z_recv.at[up, ch, step],
            device_id=(to_z * xs + x, group), device_id_type=mesh_id,
        )

    def up_out(ch, step):
        return (z + 1 < zs) & (z - step + 1 >= 0), z_copy(ch, step, 1, z - step + 1, z + 1)

    def down_out(ch, step):
        return (z >= 1) & (z + step - 1 < zs), z_copy(ch, step, 0, z + step - 1, z - 1)

    def up_in(ch, step):
        return z - step >= 0, z_copy(ch, step, 1, z - step, z - 1)

    def down_in(ch, step):
        return z + step < zs, z_copy(ch, step, 0, z + step, z + 1)

    def x_copy(ch, owner_z, owner_x, d):
        ref = gath[ch].at[pl.ds(2 * (owner_z * xs + owner_x), 2)]
        return pltpu.make_async_remote_copy(
            src_ref=ref, dst_ref=ref,
            send_sem=x_send.at[ch, owner_z, d], recv_sem=x_recv.at[ch, owner_z, d],
            device_id=(z * xs + lax.rem(x + d, xs), group), device_id_type=mesh_id,
        )

    def c_copy(ch, d):
        to = lax.rem(group + d, groups)
        return pltpu.make_async_remote_copy(
            src_ref=chosen.at[ch, to],
            dst_ref=seated.at[:, pl.ds(pl.multiple_of(group * rows + ch * part, part), part)],
            send_sem=c_send.at[ch, d], recv_sem=c_recv.at[ch, d],
            device_id=(me, to), device_id_type=mesh_id,
        )

    def share_row(ch, owner_z):
        for d in range(1, xs):
            x_copy(ch, owner_z, x, d).start()

    barrier = pltpu.get_barrier_semaphore()

    @pl.when(z >= 1)
    def _():
        pl.semaphore_signal(barrier, inc=1, device_id=(me - xs, group), device_id_type=mesh_id)

    @pl.when(z + 1 < zs)
    def _():
        pl.semaphore_signal(barrier, inc=1, device_id=(me + xs, group), device_id_type=mesh_id)

    for d in range(1, xs):
        pl.semaphore_signal(
            barrier, inc=1, device_id=(z * xs + lax.rem(x + d, xs), group), device_id_type=mesh_id
        )
    for d in range(1, groups):
        pl.semaphore_signal(
            barrier, inc=1, device_id=(me, lax.rem(group + d, groups)), device_id_type=mesh_id
        )
    for ch in range(pieces):
        for h in range(2):
            gath[ch][2 * me + h] = expr_ref[ch * part:(ch + 1) * part, h * BLOCK:(h + 1) * BLOCK]
    z_peers = lax.div(z + zs - 1, zs) + lax.div(2 * zs - 2 - z, zs)
    pl.semaphore_wait(barrier, xs + groups - 2 + z_peers)

    def begin(copy_if):
        cond, copy = copy_if

        @pl.when(cond)
        def _():
            copy.start()

    def advance(ch, step):
        if step == 0:
            begin(up_out(ch, 1))
            begin(down_out(ch, 1))
            share_row(ch, z)
            return
        for arrive, leave, owner in ((up_in, up_out, z - step), (down_in, down_out, z + step)):
            cond, copy = arrive(ch, step)

            @pl.when(cond)
            def _():
                copy.wait_recv()
                if step + 1 < zs:
                    begin(leave(ch, step + 1))
                share_row(ch, owner)

    def choose(ch):
        for owner_z in range(zs):
            for d in range(1, xs):
                x_copy(ch, owner_z, lax.rem(x + xs - d, xs), d).wait_recv()
        for c in range(groups):
            for s, seat in enumerate(seat_of(tables, me, c // split)):
                chosen[ch, c, s] = gath[ch][plan_ref[seat]]
        for d in range(1, groups):
            c_copy(ch, d).start()
        seated[:, pl.ds(pl.multiple_of(group * rows + ch * part, part), part)] = chosen[ch, group]

    def weigh(ch):
        for d in range(1, groups):
            c_copy(ch, d).wait_recv()

        @pl.loop(0, groups)
        def _(g):
            base = pl.multiple_of(g * rows + ch * part, part)
            at = pl.ds(base, part)
            turned = seated[0, at, :].astype(jnp.float32).T
            for k in range(0, BLOCK, 32):
                vals = basis(turned[k:k + 32], 1.0)
                for i in range(BINS):
                    wf[i * BLOCK + k:i * BLOCK + k + 32, at] = vals[i].astype(jnp.bfloat16)
            for k in range(0, part, 32):
                rows_at = pl.ds(base + k, 32)
                vals = basis(seated[1, rows_at, :], 1.0 / (rows * groups))
                for i in range(BINS):
                    ws[rows_at, i * BLOCK:(i + 1) * BLOCK] = vals[i].astype(jnp.bfloat16)

    for tick in range(pieces + zs + 1):
        for ch in range(pieces):
            if 0 <= tick - ch < zs:
                advance(ch, tick - ch)
        if 0 <= tick - zs < pieces:
            choose(tick - zs)
        if 0 <= tick - zs - 1 < pieces:
            weigh(tick - zs - 1)

    def multiply(j):
        part_sums[j % 2] = jnp.dot(
            wf[...], ws[:, j * 2 * BLOCK:(j + 1) * 2 * BLOCK], preferred_element_type=jnp.float32
        )

    def fold(j):
        sums = part_sums.at[j % 2]
        for g in range(0, BLOCK, 16):
            total = jnp.zeros((16, BLOCK), jnp.float32)
            right0 = total
            right1 = total
            for i in range(BINS):
                at = i * BLOCK + g
                v0 = sums[at:at + 16, :BLOCK]
                v1 = sums[at:at + 16, BLOCK:]
                total += entropy_terms(v0) + entropy_terms(v1)
                right0 += v0
                right1 += v1
                if j == 0:
                    left[at:at + 16, :] = v0 + v1
                elif j + 1 < BINS // 2:
                    left[at:at + 16, :] += v0 + v1
                else:
                    total -= entropy_terms(left[at:at + 16, :] + v0 + v1)
            total -= entropy_terms(right0) + entropy_terms(right1)
            if j == 0:
                mine[g:g + 16, :] = total
            else:
                mine[g:g + 16, :] += total

    multiply(0)
    for j in range(BINS // 2):
        if j + 1 < BINS // 2:
            multiply(j + 1)
        fold(j)

    share = out_ref.shape[1]
    turn = lax.div(group, split)

    def o_copy(k):
        to = lax.rem(group + k * split, groups)
        return pltpu.make_async_remote_copy(
            src_ref=mine.at[pl.ds(pl.multiple_of(to * share, share), share)],
            dst_ref=out_ref.at[turn],
            send_sem=o_send.at[k], recv_sem=o_recv.at[k],
            device_id=(me, to), device_id_type=mesh_id,
        )

    for k in range(1, ROUNDS):
        o_copy(k).start()
    out_ref[turn] = mine[pl.ds(pl.multiple_of(group * share, share), share), :]
    for ch in range(pieces):
        for d in range(1, groups):
            c_copy(ch, d).wait_send()
        for step in range(1, zs):
            for cond, copy in (up_out(ch, step), down_out(ch, step)):

                @pl.when(cond)
                def _():
                    copy.wait_send()
        for owner_z in range(zs):
            for d in range(1, xs):
                x_copy(ch, owner_z, x, d).wait_send()
    for k in range(1, ROUNDS):
        o_copy(k).wait()


def local(expression, plan, screen):
    tables = lax.axis_size("pair")
    groups = lax.axis_size("cell")
    rows = expression.shape[0]
    cells = rows * groups
    zs, xs = grid_of(tables)
    pieces = rows // BLOCK
    part = rows // pieces
    dma = pltpu.SemaphoreType.DMA
    values = pl.pallas_call(
        functools.partial(kernel, tables, groups, pieces),
        out_shape=jax.ShapeDtypeStruct((ROUNDS, BLOCK // groups, BLOCK), jnp.float32),
        in_specs=[
            pl.BlockSpec(memory_space=pltpu.SMEM),
            pl.BlockSpec(memory_space=pltpu.VMEM),
        ],
        out_specs=pl.BlockSpec(memory_space=pltpu.VMEM),
        scratch_shapes=[pltpu.VMEM((2 * tables, part, BLOCK), jnp.bfloat16)] * pieces
        + [
            pltpu.VMEM((pieces, groups, 2, part, BLOCK), jnp.bfloat16),
            pltpu.VMEM((2, cells, BLOCK), jnp.bfloat16),
            pltpu.VMEM((BINS * BLOCK, cells), jnp.bfloat16),
            pltpu.VMEM((cells, BINS * BLOCK), jnp.bfloat16),
            pltpu.VMEM((2, BINS * BLOCK, 2 * BLOCK), jnp.float32),
            pltpu.VMEM((BINS * BLOCK, BLOCK), jnp.float32),
            pltpu.VMEM((BLOCK, BLOCK), jnp.float32),
            dma((2, pieces, zs)),
            dma((2, pieces, zs)),
            dma((pieces, zs, xs)),
            dma((pieces, zs, xs)),
            dma((pieces, groups)),
            dma((pieces, groups)),
            dma((ROUNDS,)),
            dma((ROUNDS,)),
        ],
        compiler_params=pltpu.CompilerParams(
            collective_id=0, has_side_effects=True, vmem_limit_bytes=52 * 1024 * 1024
        ),
    )(plan, expression)
    passed = lax.dynamic_slice_in_dim(screen, lax.axis_index("pair"), 1, 1)
    return jnp.where(passed[:, :, None] == 1, values, jnp.float32(0.0))


def solution(mesh):
    return jax.shard_map(
        local,
        mesh=mesh,
        in_specs=(P("cell", "pair"), P(), P()),
        out_specs=P(None, ("pair", "cell"), None),
        check_vma=False,
    )
```
